32 devices in a mesh: row: 4 (over z), col: 8 (over y, x, core).
Axes of the slice: x: 2, y: 2, z: 4, core: 2. Of those that a mesh axis runs over, the one named last changes fastest.
Arguments:
- blocks: bfloat16 [64, 8, 128, 128], P(('row', 'col')), may hold values from -1.5 to 1.5
- colidx: int32 [64, 8], P(('row', 'col')), may hold values from 0 to 63, as said below
- counts: int32 [4, 8], P('row', 'col'), may hold values from 1 to 66, as said below
- out_list: int32 [4, 8, 66], P('row', 'col'), may hold values from 0 to 65, as said below
Outputs:
- packed: bfloat16 [2112, 128, 128], P(('row', 'col'))
- offsets: int32 [4, 8], P('row', 'col')
The draws below stay inside these ranges and needn't reach their ends.
Inputs may be any that keep to these rules, and one draw needn't show every extreme that they name: `colidx`: block row i names 8 distinct block columns (i + e) mod 64 with -8 <= e <= 8; among them are i, (i - 8) mod 64 and (i + 8) mod 64. `counts`: some device keeps all 66 blocks and some device keeps one. `out_list`: each device's list is an ordering of 0 to 65; only its first counts entries are used.
All inputs are finite; a program needn't handle non-finite values.
Results may differ from the reference program's by a relative error of at most 0.001.
Values may be sent and summed in bfloat16 or wider, within the bound.
A program may use at most 64 MiB of HBM per device.

```python
import jax
import jax.numpy as jnp
from jax import lax

BS = 128
K = 8
H = 8
BR_DEV = 2
NB = 64
TILE = 66
N_ROW = 4
N_COL = 8


def draw_colidx(key, part):
    pool_size = 2 * H - 2
    pool = jnp.concatenate([jnp.arange(1 - H, 0, dtype=jnp.int32), jnp.arange(1, H, dtype=jnp.int32)])
    scores = jax.random.randint(jax.random.fold_in(key, 5), (NB, pool_size), 0, 65536, dtype=jnp.int32)
    scores = scores * pool_size + jnp.arange(pool_size, dtype=jnp.int32)[None, :]
    order = jnp.argsort(scores, axis=-1)
    picked = jnp.take(pool, order[:, :K - 3])
    fixed = jnp.broadcast_to(jnp.array([-H, 0, H], dtype=jnp.int32)[None, :], (NB, 3))
    distances = jnp.sort(jnp.concatenate([fixed, picked], axis=1), axis=-1)
    block_rows = jnp.arange(NB, dtype=jnp.int32)[:, None]
    return ((block_rows + distances) % NB).astype(jnp.int32)


def draw_counts(key, part):
    key_values, key_high, key_low = jax.random.split(jax.random.fold_in(key, 7), 3)
    devices_all = N_ROW * N_COL
    values = jax.random.randint(key_values, (devices_all,), 1, TILE + 1, dtype=jnp.int32)
    high_spot = jax.random.randint(key_high, (), 0, devices_all, dtype=jnp.int32)
    low_spot = (high_spot + 1 + jax.random.randint(key_low, (), 0, devices_all - 1, dtype=jnp.int32)) % devices_all
    values = values.at[high_spot].set(TILE)
    values = values.at[low_spot].set(1)
    return values.reshape(N_ROW, N_COL).astype(jnp.int32)


def draw_out_list(key, part):
    scores = jax.random.randint(jax.random.fold_in(key, 11), (N_ROW, N_COL, TILE), 0, 65536, dtype=jnp.int32)
    scores = scores * TILE + jnp.arange(TILE, dtype=jnp.int32)[None, None, :]
    return jnp.argsort(scores, axis=-1).astype(jnp.int32)


def block_scale(rng, shape, cuts, low, top_value):
    loudness, own = 1.0, jax.random.fold_in(rng, 6)
    for position, shards_of in cuts:
        draws = jnp.exp(jax.random.uniform(jax.random.fold_in(own, position), (shards_of,), jnp.float32, low / len(cuts), top_value / len(cuts)))
        loudness = loudness * jnp.repeat(draws, shape[position] // shards_of).reshape([-1 if axis == position else 1 for axis in range(len(shape))])
    return loudness


def bell_draw(rng, shape, spread, bound, shards=(), kind=jnp.bfloat16):
    values = jax.random.normal(rng, shape, jnp.float32) * spread
    if len(shards) > 0:
        values = block_scale(rng, shape, shards, -0.22, 0.18) * values
    return jnp.clip(values, min=-bound, max=bound).astype(kind)


def setup_inputs(seed: int = 0) -> dict:
    keys = jax.random.split(jax.random.key(seed), 5)
    blocks = bell_draw(keys[0], (NB, K, BS, BS), 0.25, 1.5, ((0, 32),))
    colidx = draw_colidx(jax.random.fold_in(keys[4], 71), 0)
    counts = draw_counts(jax.random.fold_in(keys[4], 71), 0)
    out_list = draw_out_list(jax.random.fold_in(keys[4], 71), 0)
    return {"blocks": blocks, "colidx": colidx, "counts": counts, "out_list": out_list}


def device_packed(blocks, colidx, counts, out_list, device):
    grid_row = device // N_COL
    grid_col = device % N_COL
    first_row = device * BR_DEV
    band_size = 4 * H + 1

    def row_band(local_row):
        block_row = (first_row + local_row).astype(jnp.int32)
        a_blocks = lax.dynamic_index_in_dim(blocks, block_row, 0, keepdims=False)
        a_cols = lax.dynamic_index_in_dim(colidx, block_row, 0, keepdims=False)
        b_blocks = jnp.take(blocks, a_cols, axis=0)
        b_cols = jnp.take(colidx, a_cols, axis=0)
        products = jnp.einsum("tab,tubc->tuac", a_blocks.astype(jnp.float32), b_blocks.astype(jnp.float32),
                              precision=lax.Precision.HIGHEST)
        places = ((b_cols - block_row + 2 * H) % NB).astype(jnp.int32)
        onehot = (places[:, :, None] == jnp.arange(band_size, dtype=jnp.int32)[None, None, :]).astype(jnp.float32)
        return jnp.einsum("tuf,tuac->fac", onehot, products, precision=lax.Precision.HIGHEST)

    grid_tile = lax.map(row_band, jnp.arange(BR_DEV, dtype=jnp.int32))
    flattened = grid_tile.reshape(TILE, BS, BS)
    listing = out_list[grid_row, grid_col]
    picked = jnp.take(flattened, listing, axis=0)
    in_list = jnp.arange(TILE, dtype=jnp.int32) < counts[grid_row, grid_col]
    return jnp.where(in_list[:, None, None], picked, jnp.zeros_like(picked)).astype(jnp.bfloat16)


def reference(blocks, colidx, counts, out_list):
    indices = jnp.arange(N_ROW * N_COL, dtype=jnp.int32)
    stacked = lax.map(lambda device: device_packed(blocks, colidx, counts, out_list, device), indices)
    packed = stacked.reshape(N_ROW * N_COL * TILE, BS, BS)
    flat_counts = counts.reshape(-1)
    offsets = (jnp.cumsum(flat_counts) - flat_counts).astype(jnp.int32).reshape(N_ROW, N_COL)
    return packed, offsets
```

```python
import functools

import jax
import jax.numpy as jnp
from jax import lax
from jax.experimental import pallas as pl
from jax.experimental.pallas import tpu as pltpu
from jax.sharding import PartitionSpec as P

H = 8
CHUNKS = 4
SIDE = 4


def exchange_kernel(rows_total, cols_total, own_ref, near_ref, send_sem, recv_sem, own_sem):
    count = rows_total * cols_total
    me = lax.axis_index("row") * cols_total + lax.axis_index("col")
    core = me % 2
    pair = me // 2
    p = pair % 4
    low = p < 2
    sign = jnp.where(low, 1, -1)
    type_a = jnp.logical_or(p == 0, p == 3)
    x_step = jnp.where(p % 2 == 0, 1, -1)
    y_step = 2 * sign

    def place(device):
        return (device // cols_total, device % cols_total)

    partner = me + 1 - 2 * core
    x_dev = me + 2 * x_step
    y_dev = me + 2 * y_step
    z_to = (me + 8 * sign + count) % count
    z_from = (me - 8 * sign + count) % count

    barrier = pltpu.get_barrier_semaphore()
    for device in (partner, x_dev, y_dev, z_to, z_from):
        pl.semaphore_signal(barrier, inc=1, device_id=place(device), device_id_type=pl.DeviceIdType.MESH)
    pl.semaphore_wait(barrier, 5)

    per = near_ref.shape[1] // CHUNKS

    def part(ref, slot, c):
        return ref.at[slot, pl.ds(c * per, per)]

    def copy(source, c, lane, device, slot):
        return pltpu.make_async_remote_copy(
            src_ref=source,
            dst_ref=part(near_ref, slot, c),
            send_sem=send_sem.at[lane, c],
            recv_sem=recv_sem.at[slot, c],
            device_id=place(device),
            device_id_type=pl.DeviceIdType.MESH,
        )

    def wait_in(slot, c):
        copy(part(near_ref, slot, c), c, 0, partner, slot).wait_recv()

    def forward(slot, c, lane, device, to_slot):
        copy(part(near_ref, slot, c), c, lane, device, to_slot).start()

    own_copy = pltpu.make_async_copy(own_ref.at[0], near_ref.at[SIDE], own_sem)
    own_copy.start()

    y_slot = SIDE + 4 * sign
    z_slot = SIDE - 4 * sign
    x_slot = SIDE + 2 * x_step
    x2_slot = SIDE - 2 * x_step
    to_partner = 2 * core - 1
    for c in range(CHUNKS):
        source = part(own_ref, 0, c)
        copy(source, c, 0, y_dev, SIDE - 4 * sign).start()
        copy(source, c, 1, x_dev, SIDE - 2 * x_step).start()
    for c in range(CHUNKS):
        copy(part(own_ref, 0, c), c, 2, partner, SIDE + to_partner).start()

    y_goes = (core == 0) == low

    def y_arrived(c):
        wait_in(y_slot, c)
        forward(y_slot, c, 3, z_to, SIDE - 4 * sign)

        @pl.when(type_a)
        def _():
            forward(y_slot, c, 4, x_dev, y_slot - 2 * x_step)

        @pl.when(y_goes)
        def _():
            forward(y_slot, c, 6, partner, y_slot + to_partner)

    def x_arrived(c):
        wait_in(x_slot, c)
        forward(x_slot, c, 5, partner, x_slot + to_partner)

    def z_arrived(c):
        wait_in(z_slot, c)

        @pl.when(jnp.logical_not(type_a))
        def _():
            forward(z_slot, c, 4, x_dev, z_slot - 2 * x_step)

        @pl.when(jnp.logical_not(y_goes))
        def _():
            forward(z_slot, c, 6, partner, z_slot + to_partner)

    def x2_arrived(c):
        wait_in(x2_slot, c)
        forward(x2_slot, c, 7, partner, x2_slot + to_partner)

    for c in range(CHUNKS):
        y_arrived(c)
        x_arrived(c)
        if c > 0:
            z_arrived(c - 1)
    z_arrived(CHUNKS - 1)
    for c in range(CHUNKS):
        x2_arrived(c)
    for c in range(CHUNKS):
        for odd in (SIDE - 3, SIDE - 1, SIDE + 1, SIDE + 3):
            wait_in(odd, c)
    own_copy.wait()
    for c in range(CHUNKS):
        for lane in range(8):
            copy(part(own_ref, 0, c), c, lane, partner, SIDE).wait_send()


def exchange(blocks, mesh_shape):
    rows_here, slots, size, _ = blocks.shape
    own = blocks.reshape(1, rows_here * slots, size, size)
    near = pl.pallas_call(
        functools.partial(exchange_kernel, *mesh_shape),
        out_shape=jax.ShapeDtypeStruct((2 * SIDE + 1,) + own.shape[1:], own.dtype),
        in_specs=[pl.BlockSpec(memory_space=pl.ANY)],
        out_specs=pl.BlockSpec(memory_space=pl.ANY),
        scratch_shapes=[
            pltpu.SemaphoreType.DMA((8, CHUNKS)),
            pltpu.SemaphoreType.DMA((2 * SIDE + 1, CHUNKS)),
            pltpu.SemaphoreType.DMA,
        ],
        compiler_params=pltpu.CompilerParams(collective_id=0, has_side_effects=True),
    )(own)
    return near


def product_kernel(count, rows_here, slots, me_ref, table_ref, list_ref, near_ref, packed_ref, offset_ref, acc_ref):
    me = me_ref[0]
    width = rows_here * slots + 1
    total = count * rows_here
    band = 4 * H + 1
    first = me * rows_here
    tiles = rows_here * band

    offset_ref[0, 0] = lax.fori_loop(0, me, lambda i, s: s + table_ref[i * width + width - 1], jnp.int32(0))

    def clear(q, carry):
        acc_ref[q] = jnp.zeros(acc_ref.shape[1:], acc_ref.dtype)
        return carry

    lax.fori_loop(0, tiles, clear, 0, unroll=2)

    def wrapped(value):
        return lax.rem(value + total, total)

    def one(step, carry):
        a = step // slots
        col = table_ref[me * width + step]
        place = wrapped(col - first + SIDE * rows_here) * slots
        left = near_ref[SIDE * rows_here * slots + step]
        base = (col // rows_here) * width + (col % rows_here) * slots
        for u in range(slots):
            f = wrapped(table_ref[base + u] - (first + a) + 2 * H)
            q = a * band + f
            acc_ref[q] += jnp.dot(left, near_ref[place + u], preferred_element_type=jnp.float32)
        return carry

    lax.fori_loop(0, rows_here * slots, one, 0)

    kept = table_ref[me * width + width - 1]

    def pack(i, carry):
        q = list_ref[i]
        value = acc_ref[q].astype(packed_ref.dtype)
        packed_ref[i] = jnp.where(i < kept, value, jnp.zeros_like(value))
        return carry

    lax.fori_loop(0, tiles, pack, 0, unroll=2)


def shards(mesh_shape, blocks, colidx, counts, out_list):
    rows_here, slots, size, _ = blocks.shape
    count = mesh_shape[0] * mesh_shape[1]
    tiles = out_list.shape[-1]
    me = (lax.axis_index("row") * mesh_shape[1] + lax.axis_index("col")).astype(jnp.int32)
    meta = jnp.concatenate([colidx.reshape(-1), counts.reshape(-1)])
    table = lax.all_gather(meta, ("row", "col"), tiled=True)
    near = exchange(blocks, mesh_shape)
    near = near.reshape(-1, size, size)
    smem = pl.BlockSpec(memory_space=pltpu.SMEM)
    vmem = pl.BlockSpec(memory_space=pltpu.VMEM)
    packed, offsets = pl.pallas_call(
        functools.partial(product_kernel, count, rows_here, slots),
        out_shape=(
            jax.ShapeDtypeStruct((tiles, size, size), jnp.bfloat16),
            jax.ShapeDtypeStruct((1, 1), jnp.int32),
        ),
        in_specs=[smem, smem, smem, vmem],
        out_specs=(vmem, smem),
        scratch_shapes=[pltpu.VMEM((tiles, size, size), jnp.float32)],
        compiler_params=pltpu.CompilerParams(vmem_limit_bytes=40 * 1024 * 1024),
    )(me.reshape(1), table, out_list.reshape(-1), near)
    return packed, offsets


def solution(mesh):
    mesh_shape = (mesh.shape["row"], mesh.shape["col"])
    in_specs = (
        P(("row", "col"), None, None, None),
        P(("row", "col"), None),
        P("row", "col"),
        P("row", "col", None),
    )
    out_specs = (P(("row", "col"), None, None), P("row", "col"))
    return jax.shard_map(
        functools.partial(shards, mesh_shape), mesh=mesh, in_specs=in_specs, out_specs=out_specs, check_vma=False
    )
```

```python
import functools

import jax
import jax.numpy as jnp
from jax import lax
from jax.experimental import pallas as pl
from jax.experimental.pallas import tpu as pltpu
from jax.sharding import PartitionSpec as P

H = 8
CHUNKS = 4
SIDE = 4


def exchange_kernel(
    rows_total, cols_total, col_ref, count_ref, own_ref, near_ref, meta_ref,
    table_ref, send_sem, recv_sem, own_sem, row_send, row_recv, grid_send, grid_recv,
):
    count = rows_total * cols_total
    me = lax.axis_index("row") * cols_total + lax.axis_index("col")
    core = me % 2
    pair = me // 2
    p = pair % 4
    low = p < 2
    sign = jnp.where(low, 1, -1)
    type_a = jnp.logical_or(p == 0, p == 3)
    x_step = jnp.where(p % 2 == 0, 1, -1)
    y_step = 2 * sign

    def place(device):
        return (device // cols_total, device % cols_total)

    partner = me + 1 - 2 * core
    x_dev = me + 2 * x_step
    y_dev = me + 2 * y_step
    z_to = (me + 8 * sign + count) % count
    z_from = (me - 8 * sign + count) % count

    barrier = pltpu.get_barrier_semaphore()
    r, cc = me // cols_total, me % cols_total
    row_peers = [(r, (cc + j) % cols_total) for j in range(1, cols_total)]
    grid_peers = [((r + j) % rows_total, cc) for j in range(1, rows_total)]
    others = [] if cols_total == 8 else [place(z_to), place(z_from)]
    greeted = row_peers + grid_peers + others
    for device in greeted:
        pl.semaphore_signal(barrier, inc=1, device_id=device, device_id_type=pl.DeviceIdType.MESH)

    entries = col_ref.shape[0] * col_ref.shape[1]
    lane = lax.broadcasted_iota(jnp.int32, (1, 128), 1)
    row = jnp.where(lane == entries, count_ref[0, 0], 0)
    for i in range(entries):
        row = jnp.where(lane == i, col_ref[i // col_ref.shape[1], i % col_ref.shape[1]], row)
    table_ref[me] = row
    pl.semaphore_wait(barrier, len(greeted))

    def row_copy(j):
        return pltpu.make_async_remote_copy(
            src_ref=table_ref.at[me], dst_ref=table_ref.at[me], send_sem=row_send.at[j], recv_sem=row_recv.at[j],
            device_id=row_peers[j], device_id_type=pl.DeviceIdType.MESH)

    def grid_copy(j):
        rows = table_ref.at[pl.ds(r * cols_total, cols_total)]
        return pltpu.make_async_remote_copy(
            src_ref=rows, dst_ref=rows, send_sem=grid_send.at[j], recv_sem=grid_recv.at[j],
            device_id=grid_peers[j], device_id_type=pl.DeviceIdType.MESH)

    per = near_ref.shape[1] // CHUNKS

    def part(ref, slot, c):
        return ref.at[slot, pl.ds(c * per, per)]

    def copy(source, c, lane, device, slot):
        return pltpu.make_async_remote_copy(
            src_ref=source,
            dst_ref=part(near_ref, slot, c),
            send_sem=send_sem.at[lane, c],
            recv_sem=recv_sem.at[slot, c],
            device_id=place(device),
            device_id_type=pl.DeviceIdType.MESH,
        )

    def wait_in(slot, c):
        copy(part(near_ref, slot, c), c, 0, partner, slot).wait_recv()

    def forward(slot, c, lane, device, to_slot):
        copy(part(near_ref, slot, c), c, lane, device, to_slot).start()

    own_copy = pltpu.make_async_copy(own_ref.at[0], near_ref.at[SIDE], own_sem)
    own_copy.start()

    y_slot = SIDE + 4 * sign
    z_slot = SIDE - 4 * sign
    x_slot = SIDE + 2 * x_step
    x2_slot = SIDE - 2 * x_step
    to_partner = 2 * core - 1
    for c in range(CHUNKS):
        source = part(own_ref, 0, c)
        copy(source, c, 0, y_dev, SIDE - 4 * sign).start()
        copy(source, c, 1, x_dev, SIDE - 2 * x_step).start()
    for c in range(CHUNKS):
        copy(part(own_ref, 0, c), c, 2, partner, SIDE + to_partner).start()

    for j in range(cols_total - 1):
        row_copy(j).start()
    for j in range(cols_total - 1):
        row_copy(j).wait()
    for j in range(rows_total - 1):
        grid_copy(j).start()

    y_goes = (core == 0) == low

    def y_arrived(c):
        wait_in(y_slot, c)
        forward(y_slot, c, 3, z_to, SIDE - 4 * sign)

        @pl.when(type_a)
        def _():
            forward(y_slot, c, 4, x_dev, y_slot - 2 * x_step)

        @pl.when(y_goes)
        def _():
            forward(y_slot, c, 6, partner, y_slot + to_partner)

    def x_arrived(c):
        wait_in(x_slot, c)
        forward(x_slot, c, 5, partner, x_slot + to_partner)

    def z_arrived(c):
        wait_in(z_slot, c)

        @pl.when(jnp.logical_not(type_a))
        def _():
            forward(z_slot, c, 4, x_dev, z_slot - 2 * x_step)

        @pl.when(jnp.logical_not(y_goes))
        def _():
            forward(z_slot, c, 6, partner, z_slot + to_partner)

    def x2_arrived(c):
        wait_in(x2_slot, c)
        forward(x2_slot, c, 7, partner, x2_slot + to_partner)

    for c in range(CHUNKS):
        y_arrived(c)
        x_arrived(c)
        if c > 0:
            z_arrived(c - 1)
    z_arrived(CHUNKS - 1)
    for c in range(CHUNKS):
        x2_arrived(c)
    for c in range(CHUNKS):
        for odd in (SIDE - 3, SIDE - 1, SIDE + 1, SIDE + 3):
            wait_in(odd, c)
    own_copy.wait()
    for j in range(rows_total - 1):
        grid_copy(j).wait()
    for k in range(2 * SIDE + 1):
        meta_ref[k] = table_ref[(me + k - SIDE + count) % count]
    index = lax.broadcasted_iota(jnp.int32, (count, 1, 128), 0)
    meta_ref[2 * SIDE + 1] = jnp.sum(jnp.where(index < me, table_ref[...], 0), axis=0)
    for c in range(CHUNKS):
        for lane in range(8):
            copy(part(own_ref, 0, c), c, lane, partner, SIDE).wait_send()


def exchange(blocks, colidx, counts, mesh_shape):
    rows_here, slots, size, _ = blocks.shape
    own = blocks.reshape(1, rows_here * slots, size, size)
    rows_total, cols_total = mesh_shape
    smem = pl.BlockSpec(memory_space=pltpu.SMEM)
    vmem = pl.BlockSpec(memory_space=pltpu.VMEM)
    return pl.pallas_call(
        functools.partial(exchange_kernel, *mesh_shape),
        out_shape=(
            pltpu.VMEM((2 * SIDE + 1,) + own.shape[1:], own.dtype),
            jax.ShapeDtypeStruct((2 * SIDE + 2, 1, 128), jnp.int32),
        ),
        in_specs=[smem, smem, pl.BlockSpec(memory_space=pl.ANY)],
        out_specs=(vmem, vmem),
        scratch_shapes=[
            pltpu.VMEM((rows_total * cols_total, 1, 128), jnp.int32),
            pltpu.SemaphoreType.DMA((8, CHUNKS)),
            pltpu.SemaphoreType.DMA((2 * SIDE + 1, CHUNKS)),
            pltpu.SemaphoreType.DMA,
            pltpu.SemaphoreType.DMA((cols_total - 1,)),
            pltpu.SemaphoreType.DMA((cols_total - 1,)),
            pltpu.SemaphoreType.DMA((rows_total - 1,)),
            pltpu.SemaphoreType.DMA((rows_total - 1,)),
        ],
        compiler_params=pltpu.CompilerParams(collective_id=0, has_side_effects=True, vmem_limit_bytes=16 * 1024 * 1024),
    )(colidx, counts, own)


def product_kernel(count, rows_here, slots, me_ref, meta_ref, list_ref, near_ref, packed_ref, offset_ref, acc_ref):
    me = me_ref[0]
    entries = rows_here * slots
    total = count * rows_here
    band = 4 * H + 1
    first = me * rows_here
    tiles = rows_here * band
    size = acc_ref.shape[1]

    offset_ref[0, 0] = meta_ref[2 * SIDE + 1, 0, entries]

    def clear(q, carry):
        acc_ref[q] = jnp.zeros(acc_ref.shape[1:], acc_ref.dtype)
        return carry

    lax.fori_loop(0, tiles, clear, 0, unroll=6)

    def wrapped(value):
        return lax.rem(value + total, total)

    def one(step, carry):
        a = step // slots
        col = meta_ref[SIDE, 0, step]
        place = wrapped(col - first + SIDE * rows_here)
        left = near_ref[SIDE, step]
        source = place // rows_here
        base = (place % rows_here) * slots
        products = [
            jnp.dot(left, near_ref[source, base + u], preferred_element_type=jnp.float32) for u in range(slots)
        ]
        for u in range(slots):
            f = wrapped(meta_ref[source, 0, base + u] - (first + a) + 2 * H)
            acc_ref[a * band + f] += products[u]
        return carry

    lax.fori_loop(0, entries, one, 0)

    kept = meta_ref[SIDE, 0, entries]

    def pack(i, carry):
        q = list_ref[0, 0, i]
        value = acc_ref[q].astype(packed_ref.dtype)
        packed_ref[i] = jnp.where(i < kept, value, jnp.zeros_like(value))
        return carry

    lax.fori_loop(0, tiles, pack, 0, unroll=6)


def shards(mesh_shape, blocks, colidx, counts, out_list):
    rows_here, slots, size, _ = blocks.shape
    count = mesh_shape[0] * mesh_shape[1]
    tiles = out_list.shape[-1]
    me = (lax.axis_index("row") * mesh_shape[1] + lax.axis_index("col")).astype(jnp.int32)
    near, meta = exchange(blocks, colidx, counts, mesh_shape)
    smem = pl.BlockSpec(memory_space=pltpu.SMEM)
    vmem = pl.BlockSpec(memory_space=pltpu.VMEM)
    packed, offsets = pl.pallas_call(
        functools.partial(product_kernel, count, rows_here, slots),
        out_shape=(
            jax.ShapeDtypeStruct((tiles, size, size), jnp.bfloat16),
            jax.ShapeDtypeStruct((1, 1), jnp.int32),
        ),
        in_specs=[smem, smem, smem, vmem],
        out_specs=(vmem, smem),
        scratch_shapes=[pltpu.VMEM((tiles, size, size), jnp.float32)],
        compiler_params=pltpu.CompilerParams(vmem_limit_bytes=32 * 1024 * 1024),
    )(me.reshape(1), meta, out_list, near)
    return packed, offsets


def solution(mesh):
    mesh_shape = (mesh.shape["row"], mesh.shape["col"])
    in_specs = (
        P(("row", "col"), None, None, None),
        P(("row", "col"), None),
        P("row", "col"),
        P("row", "col", None),
    )
    out_specs = (P(("row", "col"), None, None), P("row", "col"))
    return jax.shard_map(
        functools.partial(shards, mesh_shape), mesh=mesh, in_specs=in_specs, out_specs=out_specs, check_vma=False
    )
```

```python
import functools

import jax
import jax.numpy as jnp
from jax import lax
from jax.experimental import pallas as pl
from jax.experimental.pallas import tpu as pltpu
from jax.sharding import PartitionSpec as P

H = 8
CHUNKS = 4
HALF = CHUNKS // 2
X_ORDER = tuple(range(HALF, CHUNKS)) + tuple(range(HALF))
SIDE = 4


def exchange_kernel(
    rows_total, cols_total, col_hbm, count_ref, own_ref, near_ref, meta_ref,
    table_ref, relay_ref, col_ref, send_sem, recv_sem, relay_sem, own_sem, col_sem, row_send, row_recv, grid_send, grid_recv,
):
    col_copy = pltpu.make_async_copy(col_hbm, col_ref, col_sem)
    col_copy.start()
    count = rows_total * cols_total
    me = lax.axis_index("row") * cols_total + lax.axis_index("col")
    core = me % 2
    pair = me // 2
    p = pair % 4
    low = p < 2
    sign = jnp.where(low, 1, -1)
    type_a = jnp.logical_or(p == 0, p == 3)
    x_step = jnp.where(p % 2 == 0, 1, -1)
    y_step = 2 * sign

    def place(device):
        return (device // cols_total, device % cols_total)

    partner = me + 1 - 2 * core
    x_dev = me + 2 * x_step
    y_dev = me + 2 * y_step
    z_to = (me + 8 * sign + count) % count
    z_from = (me - 8 * sign + count) % count

    barrier = pltpu.get_barrier_semaphore()
    r, cc = me // cols_total, me % cols_total
    row_peers = [(r, (cc + j) % cols_total) for j in range(1, cols_total)]
    grid_peers = [((r + j) % rows_total, cc) for j in range(1, rows_total)]
    others = [] if cols_total == 8 else [place(z_to), place(z_from)]
    greeted = row_peers + grid_peers + others
    for device in greeted:
        pl.semaphore_signal(barrier, inc=1, device_id=device, device_id_type=pl.DeviceIdType.MESH)

    own_copy = pltpu.make_async_copy(own_ref.at[0], near_ref.at[SIDE], own_sem)
    own_copy.start()
    col_copy.wait()
    entries = col_ref.shape[0] * col_ref.shape[1]
    lane = lax.broadcasted_iota(jnp.int32, (1, 128), 1)
    row = jnp.where(lane == entries, count_ref[0, 0], 0)
    for i in range(entries):
        row = jnp.where(lane == i, col_ref[i // col_ref.shape[1], i % col_ref.shape[1]], row)
    table_ref[me] = row
    pl.semaphore_wait(barrier, len(greeted))

    def row_copy(j):
        return pltpu.make_async_remote_copy(
            src_ref=table_ref.at[me], dst_ref=table_ref.at[me], send_sem=row_send.at[j], recv_sem=row_recv.at[j],
            device_id=row_peers[j], device_id_type=pl.DeviceIdType.MESH)

    def grid_copy(j):
        rows = table_ref.at[pl.ds(r * cols_total, cols_total)]
        return pltpu.make_async_remote_copy(
            src_ref=rows, dst_ref=rows, send_sem=grid_send.at[j], recv_sem=grid_recv.at[j],
            device_id=grid_peers[j], device_id_type=pl.DeviceIdType.MESH)

    per = near_ref.shape[1] // CHUNKS

    def part(ref, slot, c):
        return ref.at[slot, pl.ds(c * per, per)]

    def copy(source, c, lane, device, slot):
        return pltpu.make_async_remote_copy(
            src_ref=source,
            dst_ref=part(near_ref, slot, c),
            send_sem=send_sem.at[lane, c],
            recv_sem=recv_sem.at[slot, c],
            device_id=place(device),
            device_id_type=pl.DeviceIdType.MESH,
        )

    def wait_in(slot, c):
        copy(part(near_ref, slot, c), c, 0, partner, slot).wait_recv()

    def forward(slot, c, lane, device, to_slot):
        copy(part(near_ref, slot, c), c, lane, device, to_slot).start()

    y_slot = SIDE + 4 * sign
    z_slot = SIDE - 4 * sign
    x_slot = SIDE + 2 * x_step
    x2_slot = SIDE - 2 * x_step
    to_partner = 2 * core - 1
    for j in range(cols_total - 1):
        row_copy(j).start()
    for i in range(CHUNKS):
        copy(part(own_ref, 0, i), i, 0, y_dev, SIDE - 4 * sign).start()
        c = X_ORDER[i]
        copy(part(own_ref, 0, c), c, 1, x_dev, SIDE - 2 * x_step).start()
    for c in range(CHUNKS):
        copy(part(own_ref, 0, c), c, 2, partner, SIDE + to_partner).start()

    y_goes = (core == 0) == low

    def y_arrived(c):
        wait_in(y_slot, c)
        forward(y_slot, c, 3, z_to, SIDE - 4 * sign)

        if c < HALF:
            @pl.when(type_a)
            def _():
                forward(y_slot, c, 4, x_dev, y_slot - 2 * x_step)

        @pl.when(y_goes)
        def _():
            forward(y_slot, c, 6, partner, y_slot + to_partner)

    def relay(c, lane, device):
        return pltpu.make_async_remote_copy(
            src_ref=part(near_ref, x_slot, c), dst_ref=relay_ref.at[c - HALF], send_sem=send_sem.at[lane, c],
            recv_sem=relay_sem.at[c - HALF], device_id=place(device), device_id_type=pl.DeviceIdType.MESH)

    def x_arrived(c):
        wait_in(x_slot, c)
        if c >= HALF:
            @pl.when(type_a)
            def _():
                forward(x_slot, c, 8, y_dev, x_slot - 2 * y_step)

            @pl.when(jnp.logical_not(type_a))
            def _():
                relay(c, 8, z_from).start()
        forward(x_slot, c, 5, partner, x_slot + to_partner)

    def z_arrived(c):
        wait_in(z_slot, c)

        if c < HALF:
            @pl.when(jnp.logical_not(type_a))
            def _():
                forward(z_slot, c, 4, x_dev, z_slot - 2 * x_step)

        @pl.when(jnp.logical_not(y_goes))
        def _():
            forward(z_slot, c, 6, partner, z_slot + to_partner)

    def relay_arrived(c):
        @pl.when(jnp.logical_not(type_a))
        def _():
            relay(c, 8, z_from).wait_recv()
            copy(relay_ref.at[c - HALF], c, 9, y_dev, SIDE - 2 * x_step).start()

    def x2_arrived(c):
        wait_in(x2_slot, c)
        forward(x2_slot, c, 7, partner, x2_slot + to_partner)

    for i in range(CHUNKS):
        y_arrived(i)
        x_arrived(X_ORDER[i])
        if i > 0:
            z_arrived(i - 1)
            if i <= HALF:
                relay_arrived(HALF + i - 1)
        if i == 1:
            for j in range(cols_total - 1):
                row_copy(j).wait()
            for j in range(rows_total - 1):
                grid_copy(j).start()
    z_arrived(CHUNKS - 1)
    for c in range(HALF):
        x2_arrived(c)
        x2_arrived(c + HALF)
    for c in range(CHUNKS):
        for odd in (SIDE - 3, SIDE - 1, SIDE + 1, SIDE + 3):
            wait_in(odd, c)
    own_copy.wait()
    for j in range(rows_total - 1):
        grid_copy(j).wait()
    for k in range(2 * SIDE + 1):
        meta_ref[k] = table_ref[(me + k - SIDE + count) % count]
    index = lax.broadcasted_iota(jnp.int32, (count, 1, 128), 0)
    meta_ref[2 * SIDE + 1] = jnp.sum(jnp.where(index < me, table_ref[...], 0), axis=0)
    for c in range(CHUNKS):
        for lane in (0, 1, 2, 3, 5, 6, 7, 4 if c < HALF else 8):
            copy(part(own_ref, 0, c), c, lane, partner, SIDE).wait_send()

    @pl.when(jnp.logical_not(type_a))
    def _():
        for c in range(HALF, CHUNKS):
            copy(part(own_ref, 0, c), c, 9, partner, SIDE).wait_send()


def exchange(blocks, colidx, counts, mesh_shape):
    rows_here, slots, size, _ = blocks.shape
    own = blocks.reshape(1, rows_here * slots, size, size)
    rows_total, cols_total = mesh_shape
    smem = pl.BlockSpec(memory_space=pltpu.SMEM)
    vmem = pl.BlockSpec(memory_space=pltpu.VMEM)
    hbm = pl.BlockSpec(memory_space=pltpu.HBM)
    return pl.pallas_call(
        functools.partial(exchange_kernel, *mesh_shape),
        out_shape=(
            pltpu.VMEM((2 * SIDE + 1,) + own.shape[1:], own.dtype),
            jax.ShapeDtypeStruct((2 * SIDE + 2, 1, 128), jnp.int32),
        ),
        in_specs=[hbm, smem, hbm],
        out_specs=(vmem, vmem),
        scratch_shapes=[
            pltpu.VMEM((rows_total * cols_total, 1, 128), jnp.int32),
            pltpu.VMEM((CHUNKS - HALF, rows_here * slots // CHUNKS, size, size), own.dtype),
            pltpu.SMEM((rows_here, slots), jnp.int32),
            pltpu.SemaphoreType.DMA((10, CHUNKS)),
            pltpu.SemaphoreType.DMA((2 * SIDE + 1, CHUNKS)),
            pltpu.SemaphoreType.DMA((CHUNKS - HALF,)),
            pltpu.SemaphoreType.DMA,
            pltpu.SemaphoreType.DMA,
            pltpu.SemaphoreType.DMA((cols_total - 1,)),
            pltpu.SemaphoreType.DMA((cols_total - 1,)),
            pltpu.SemaphoreType.DMA((rows_total - 1,)),
            pltpu.SemaphoreType.DMA((rows_total - 1,)),
        ],
        compiler_params=pltpu.CompilerParams(collective_id=0, has_side_effects=True, vmem_limit_bytes=16 * 1024 * 1024),
    )(pltpu.with_memory_space_constraint(colidx, pltpu.HBM), counts, pltpu.with_memory_space_constraint(own, pltpu.HBM))


def product_kernel(count, rows_here, slots, me_ref, meta_ref, list_hbm, near_ref, packed_ref, offset_ref, acc_ref, list_ref, list_sem):
    list_copy = pltpu.make_async_copy(list_hbm, list_ref, list_sem)
    list_copy.start()
    me = me_ref[0]
    entries = rows_here * slots
    total = count * rows_here
    band = 4 * H + 1
    first = me * rows_here
    tiles = rows_here * band
    size = acc_ref.shape[1]

    offset_ref[0, 0] = meta_ref[2 * SIDE + 1, 0, entries]

    def clear(q, carry):
        acc_ref[q] = jnp.zeros(acc_ref.shape[1:], acc_ref.dtype)
        return carry

    lax.fori_loop(0, tiles, clear, 0, unroll=6)

    def wrapped(value):
        return lax.rem(value + total, total)

    def one(step, carry):
        a = step // slots
        col = meta_ref[SIDE, 0, step]
        place = wrapped(col - first + SIDE * rows_here)
        left = near_ref[SIDE, step]
        source = place // rows_here
        base = (place % rows_here) * slots
        right = jnp.concatenate([near_ref[source, base + u] for u in range(slots)], axis=1)
        product = jnp.dot(left, right, preferred_element_type=jnp.float32)
        for u in range(slots):
            f = wrapped(meta_ref[source, 0, base + u] - (first + a) + 2 * H)
            acc_ref[a * band + f] += product[:, u * size:(u + 1) * size]
        return carry

    lax.fori_loop(0, entries, one, 0)

    list_copy.wait()
    kept = meta_ref[SIDE, 0, entries]

    def pack(i, carry):
        q = list_ref[0, 0, i]
        value = acc_ref[q].astype(packed_ref.dtype)
        packed_ref[i] = jnp.where(i < kept, value, jnp.zeros_like(value))
        return carry

    lax.fori_loop(0, tiles, pack, 0, unroll=6)


def shards(mesh_shape, blocks, colidx, counts, out_list):
    rows_here, slots, size, _ = blocks.shape
    count = mesh_shape[0] * mesh_shape[1]
    tiles = out_list.shape[-1]
    me = (lax.axis_index("row") * mesh_shape[1] + lax.axis_index("col")).astype(jnp.int32)
    near, meta = exchange(blocks, colidx, counts, mesh_shape)
    smem = pl.BlockSpec(memory_space=pltpu.SMEM)
    vmem = pl.BlockSpec(memory_space=pltpu.VMEM)
    packed, offsets = pl.pallas_call(
        functools.partial(product_kernel, count, rows_here, slots),
        out_shape=(
            jax.ShapeDtypeStruct((tiles, size, size), jnp.bfloat16),
            jax.ShapeDtypeStruct((1, 1), jnp.int32),
        ),
        in_specs=[smem, smem, pl.BlockSpec(memory_space=pltpu.HBM), vmem],
        out_specs=(vmem, smem),
        scratch_shapes=[
            pltpu.VMEM((tiles, size, size), jnp.float32),
            pltpu.SMEM(out_list.shape, jnp.int32),
            pltpu.SemaphoreType.DMA,
        ],
        compiler_params=pltpu.CompilerParams(vmem_limit_bytes=32 * 1024 * 1024),
    )(me.reshape(1), meta, pltpu.with_memory_space_constraint(out_list, pltpu.HBM), near)
    return packed, offsets


def solution(mesh):
    mesh_shape = (mesh.shape["row"], mesh.shape["col"])
    in_specs = (
        P(("row", "col"), None, None, None),
        P(("row", "col"), None),
        P("row", "col"),
        P("row", "col", None),
    )
    out_specs = (P(("row", "col"), None, None), P("row", "col"))
    return jax.shard_map(
        functools.partial(shards, mesh_shape), mesh=mesh, in_specs=in_specs, out_specs=out_specs, check_vma=False
    )
```

```python
import functools

import jax
import jax.numpy as jnp
from jax import lax
from jax.experimental import pallas as pl
from jax.experimental.pallas import tpu as pltpu
from jax.sharding import PartitionSpec as P

H = 8
CHUNKS = 4
HALF = CHUNKS // 2
X_ORDER = tuple(range(HALF, CHUNKS)) + tuple(range(HALF))
SIDE = 4


def exchange_kernel(
    rows_total, cols_total, col_hbm, count_ref, own_ref, near_ref, meta_ref,
    table_ref, relay_ref, col_ref, send_sem, recv_sem, relay_sem, own_sem, col_sem, row_send, row_recv, grid_send, grid_recv,
):
    col_copy = pltpu.make_async_copy(col_hbm, col_ref, col_sem)
    col_copy.start()
    count = rows_total * cols_total
    me = lax.axis_index("row") * cols_total + lax.axis_index("col")
    core = me % 2
    pair = me // 2
    p = pair % 4
    low = p < 2
    sign = jnp.where(low, 1, -1)
    type_a = jnp.logical_or(p == 0, p == 3)
    x_step = jnp.where(p % 2 == 0, 1, -1)
    y_step = 2 * sign

    def place(device):
        return (device // cols_total, device % cols_total)

    partner = me + 1 - 2 * core
    x_dev = me + 2 * x_step
    y_dev = me + 2 * y_step
    z_to = (me + 8 * sign + count) % count
    z_from = (me - 8 * sign + count) % count

    barrier = pltpu.get_barrier_semaphore()
    r, cc = me // cols_total, me % cols_total
    row_peers = [(r, (cc + j) % cols_total) for j in range(1, cols_total)]
    grid_peers = [((r + j) % rows_total, cc) for j in range(1, rows_total)]
    others = [] if cols_total == 8 else [place(z_to), place(z_from)]
    greeted = row_peers + grid_peers + others
    for device in greeted:
        pl.semaphore_signal(barrier, inc=1, device_id=device, device_id_type=pl.DeviceIdType.MESH)

    own_copy = pltpu.make_async_copy(own_ref.at[0], near_ref.at[SIDE], own_sem)
    own_copy.start()
    col_copy.wait()
    entries = col_ref.shape[0] * col_ref.shape[1]
    lane = lax.broadcasted_iota(jnp.int32, (1, 128), 1)
    row = jnp.where(lane == entries, count_ref[0, 0], 0)
    for i in range(entries):
        row = jnp.where(lane == i, col_ref[i // col_ref.shape[1], i % col_ref.shape[1]], row)
    table_ref[me] = row
    pl.semaphore_wait(barrier, len(greeted))

    def row_copy(j):
        return pltpu.make_async_remote_copy(
            src_ref=table_ref.at[me], dst_ref=table_ref.at[me], send_sem=row_send.at[j], recv_sem=row_recv.at[j],
            device_id=row_peers[j], device_id_type=pl.DeviceIdType.MESH)

    def grid_copy(j):
        rows = table_ref.at[pl.ds(r * cols_total, cols_total)]
        return pltpu.make_async_remote_copy(
            src_ref=rows, dst_ref=rows, send_sem=grid_send.at[j], recv_sem=grid_recv.at[j],
            device_id=grid_peers[j], device_id_type=pl.DeviceIdType.MESH)

    per = near_ref.shape[1] // CHUNKS

    def part(ref, slot, c):
        return ref.at[slot, pl.ds(c * per, per)]

    def copy(source, c, lane, device, slot):
        return pltpu.make_async_remote_copy(
            src_ref=source,
            dst_ref=part(near_ref, slot, c),
            send_sem=send_sem.at[lane, c],
            recv_sem=recv_sem.at[slot, c],
            device_id=place(device),
            device_id_type=pl.DeviceIdType.MESH,
        )

    def wait_in(slot, c):
        copy(part(near_ref, slot, c), c, 0, partner, slot).wait_recv()

    def forward(slot, c, lane, device, to_slot):
        copy(part(near_ref, slot, c), c, lane, device, to_slot).start()

    y_slot = SIDE + 4 * sign
    z_slot = SIDE - 4 * sign
    x_slot = SIDE + 2 * x_step
    x2_slot = SIDE - 2 * x_step
    to_partner = 2 * core - 1
    for j in range(cols_total - 1):
        row_copy(j).start()
    for i in range(CHUNKS):
        copy(part(own_ref, 0, i), i, 0, y_dev, SIDE - 4 * sign).start()
        c = X_ORDER[i]
        copy(part(own_ref, 0, c), c, 1, x_dev, SIDE - 2 * x_step).start()
    for c in range(CHUNKS):
        copy(part(own_ref, 0, c), c, 2, partner, SIDE + to_partner).start()

    y_goes = (core == 0) == low

    def y_arrived(c):
        wait_in(y_slot, c)
        forward(y_slot, c, 3, z_to, SIDE - 4 * sign)

        if c < HALF:
            @pl.when(type_a)
            def _():
                forward(y_slot, c, 4, x_dev, y_slot - 2 * x_step)

        @pl.when(y_goes)
        def _():
            forward(y_slot, c, 6, partner, y_slot + to_partner)

    def relay(c, lane, device):
        return pltpu.make_async_remote_copy(
            src_ref=part(near_ref, x_slot, c), dst_ref=relay_ref.at[c - HALF], send_sem=send_sem.at[lane, c],
            recv_sem=relay_sem.at[c - HALF], device_id=place(device), device_id_type=pl.DeviceIdType.MESH)

    def x_arrived(c):
        wait_in(x_slot, c)
        if c >= HALF:
            @pl.when(type_a)
            def _():
                forward(x_slot, c, 8, y_dev, x_slot - 2 * y_step)

            @pl.when(jnp.logical_not(type_a))
            def _():
                relay(c, 8, z_from).start()
        forward(x_slot, c, 5, partner, x_slot + to_partner)

    def z_arrived(c):
        wait_in(z_slot, c)

        if c < HALF:
            @pl.when(jnp.logical_not(type_a))
            def _():
                forward(z_slot, c, 4, x_dev, z_slot - 2 * x_step)

        @pl.when(jnp.logical_not(y_goes))
        def _():
            forward(z_slot, c, 6, partner, z_slot + to_partner)

    def relay_arrived(c):
        @pl.when(jnp.logical_not(type_a))
        def _():
            relay(c, 8, z_from).wait_recv()
            copy(relay_ref.at[c - HALF], c, 9, y_dev, SIDE - 2 * x_step).start()

    def x2_arrived(c):
        wait_in(x2_slot, c)
        forward(x2_slot, c, 7, partner, x2_slot + to_partner)

    for i in range(CHUNKS):
        y_arrived(i)
        x_arrived(X_ORDER[i])
        if i > 0:
            z_arrived(i - 1)
            if i <= HALF:
                relay_arrived(HALF + i - 1)
        if i == 1:
            for j in range(cols_total - 1):
                row_copy(j).wait()
            for j in range(rows_total - 1):
                grid_copy(j).start()
    z_arrived(CHUNKS - 1)
    for c in range(HALF):
        x2_arrived(c)
        x2_arrived(c + HALF)
    for c in range(CHUNKS):
        for odd in (SIDE - 3, SIDE - 1, SIDE + 1, SIDE + 3):
            wait_in(odd, c)
    own_copy.wait()
    for j in range(rows_total - 1):
        grid_copy(j).wait()
    for k in range(2 * SIDE + 1):
        meta_ref[k] = table_ref[(me + k - SIDE + count) % count]
    index = lax.broadcasted_iota(jnp.int32, (count, 1, 128), 0)
    meta_ref[2 * SIDE + 1] = jnp.sum(jnp.where(index < me, table_ref[...], 0), axis=0)
    for c in range(CHUNKS):
        for lane in (0, 1, 2, 3, 5, 6, 7, 4 if c < HALF else 8):
            copy(part(own_ref, 0, c), c, lane, partner, SIDE).wait_send()

    @pl.when(jnp.logical_not(type_a))
    def _():
        for c in range(HALF, CHUNKS):
            copy(part(own_ref, 0, c), c, 9, partner, SIDE).wait_send()


def exchange(blocks, colidx, counts, mesh_shape):
    rows_here, slots, size, _ = blocks.shape
    own = blocks.reshape(1, rows_here * slots, size, size)
    rows_total, cols_total = mesh_shape
    smem = pl.BlockSpec(memory_space=pltpu.SMEM)
    vmem = pl.BlockSpec(memory_space=pltpu.VMEM)
    hbm = pl.BlockSpec(memory_space=pltpu.HBM)
    return pl.pallas_call(
        functools.partial(exchange_kernel, *mesh_shape),
        out_shape=(
            pltpu.VMEM((2 * SIDE + 1,) + own.shape[1:], own.dtype),
            jax.ShapeDtypeStruct((2 * SIDE + 2, 1, 128), jnp.int32),
        ),
        in_specs=[hbm, smem, hbm],
        out_specs=(vmem, vmem),
        scratch_shapes=[
            pltpu.VMEM((rows_total * cols_total, 1, 128), jnp.int32),
            pltpu.VMEM((CHUNKS - HALF, rows_here * slots // CHUNKS, size, size), own.dtype),
            pltpu.SMEM((rows_here, slots), jnp.int32),
            pltpu.SemaphoreType.DMA((10, CHUNKS)),
            pltpu.SemaphoreType.DMA((2 * SIDE + 1, CHUNKS)),
            pltpu.SemaphoreType.DMA((CHUNKS - HALF,)),
            pltpu.SemaphoreType.DMA,
            pltpu.SemaphoreType.DMA,
            pltpu.SemaphoreType.DMA((cols_total - 1,)),
            pltpu.SemaphoreType.DMA((cols_total - 1,)),
            pltpu.SemaphoreType.DMA((rows_total - 1,)),
            pltpu.SemaphoreType.DMA((rows_total - 1,)),
        ],
        compiler_params=pltpu.CompilerParams(collective_id=0, has_side_effects=True, vmem_limit_bytes=16 * 1024 * 1024),
    )(pltpu.with_memory_space_constraint(colidx, pltpu.HBM), counts, pltpu.with_memory_space_constraint(own, pltpu.HBM))


def product_kernel(
    count, rows_here, slots, me_ref, meta_vmem, list_hbm, near_ref, packed_ref, offset_ref,
    acc_ref, out_ref, meta_ref, list_ref, meta_sem, list_sem, out_sem,
):
    meta_copy = pltpu.make_async_copy(meta_vmem, meta_ref, meta_sem)
    meta_copy.start()
    list_copy = pltpu.make_async_copy(list_hbm, list_ref, list_sem)
    list_copy.start()
    me = me_ref[0]
    entries = rows_here * slots
    total = count * rows_here
    band = 4 * H + 1
    first = me * rows_here
    tiles = rows_here * band
    size = acc_ref.shape[1]

    def clear(q, carry):
        acc_ref[q] = jnp.zeros(acc_ref.shape[1:], acc_ref.dtype)
        return carry

    lax.fori_loop(0, tiles, clear, 0, unroll=6)

    meta_copy.wait()
    offset_ref[0, 0] = meta_ref[2 * SIDE + 1, 0, entries]

    def wrapped(value):
        return lax.rem(value + total, total)

    def one(step, carry):
        a = step // slots
        col = meta_ref[SIDE, 0, step]
        place = wrapped(col - first + SIDE * rows_here)
        left = near_ref[SIDE, step]
        source = place // rows_here
        base = (place % rows_here) * slots
        right = jnp.concatenate([near_ref[source, base + u] for u in range(slots)], axis=1)
        product = jnp.dot(left, right, preferred_element_type=jnp.float32)
        for u in range(slots):
            f = wrapped(meta_ref[source, 0, base + u] - (first + a) + 2 * H)
            acc_ref[a * band + f] += product[:, u * size:(u + 1) * size]
        return carry

    lax.fori_loop(0, entries, one, 0, unroll=True)

    list_copy.wait()
    kept = meta_ref[SIDE, 0, entries]

    def pack(i, carry):
        q = list_ref[0, 0, i]
        value = acc_ref[q].astype(out_ref.dtype)
        out_ref[i] = jnp.where(i < kept, value, jnp.zeros_like(value))
        return carry

    group = band // 3
    writes = []
    for g in range(tiles // group):
        lax.fori_loop(g * group, (g + 1) * group, pack, 0, unroll=True)
        span = pl.ds(g * group, group)
        writes.append(pltpu.make_async_copy(out_ref.at[span], packed_ref.at[span], out_sem.at[g]))
        writes[-1].start()
    for write in writes:
        write.wait()


def shards(mesh_shape, blocks, colidx, counts, out_list):
    rows_here, slots, size, _ = blocks.shape
    count = mesh_shape[0] * mesh_shape[1]
    tiles = out_list.shape[-1]
    me = (lax.axis_index("row") * mesh_shape[1] + lax.axis_index("col")).astype(jnp.int32)
    near, meta = exchange(blocks, colidx, counts, mesh_shape)
    smem = pl.BlockSpec(memory_space=pltpu.SMEM)
    vmem = pl.BlockSpec(memory_space=pltpu.VMEM)
    hbm = pl.BlockSpec(memory_space=pltpu.HBM)
    packed, offsets = pl.pallas_call(
        functools.partial(product_kernel, count, rows_here, slots),
        out_shape=(
            jax.ShapeDtypeStruct((tiles, size, size), jnp.bfloat16),
            jax.ShapeDtypeStruct((1, 1), jnp.int32),
        ),
        in_specs=[smem, vmem, hbm, vmem],
        out_specs=(hbm, smem),
        scratch_shapes=[
            pltpu.VMEM((tiles, size, size), jnp.float32),
            pltpu.VMEM((tiles, size, size), jnp.bfloat16),
            pltpu.SMEM(meta.shape, jnp.int32),
            pltpu.SMEM(out_list.shape, jnp.int32),
            pltpu.SemaphoreType.DMA,
            pltpu.SemaphoreType.DMA,
            pltpu.SemaphoreType.DMA((3 * rows_here,)),
        ],
        compiler_params=pltpu.CompilerParams(vmem_limit_bytes=32 * 1024 * 1024),
    )(me.reshape(1), meta, pltpu.with_memory_space_constraint(out_list, pltpu.HBM), near)
    return packed, offsets


def solution(mesh):
    mesh_shape = (mesh.shape["row"], mesh.shape["col"])
    in_specs = (
        P(("row", "col"), None, None, None),
        P(("row", "col"), None),
        P("row", "col"),
        P("row", "col", None),
    )
    out_specs = (P(("row", "col"), None, None), P("row", "col"))
    return jax.shard_map(
        functools.partial(shards, mesh_shape), mesh=mesh, in_specs=in_specs, out_specs=out_specs, check_vma=False
    )
```
